32 devices in a mesh: space: 8 (over z, y), chan: 4 (over x, core).
Axes of the slice: x: 2, y: 2, z: 4, core: 2. Of those that a mesh axis runs over, the one named last changes fastest.
Arguments:
- fine_tiles: bfloat16 [256, 96, 512], P('space', 'chan'), may hold values from -6 to 6
- parent_route: int32 [256, 1], P('space'), may hold values from 0 to 7; in each aligned block of 32 rows (0 to 31, 32 to 63, ...) at most 8 rows name the same one
- parent_slots: int32 [64, 8], P('space'), may hold values from 0 to 63, as said below
- w_down: bfloat16 [8, 96, 192], replicated, may hold values from -0.21875 to 0.21875
- coarse_bias: float32 [192], replicated, may hold values from -4 to 4
- w_mid: bfloat16 [192, 192], replicated, may hold values from -0.4375 to 0.4375
- w_up: bfloat16 [8, 192, 96], replicated, may hold values from -0.4375 to 0.4375
Outputs:
- fine_out: bfloat16 [256, 96, 512], P('space', 'chan')
The draws below stay inside these ranges and needn't reach their ends.
Inputs may be any that keep to these rules, and one draw needn't show every extreme that they name: `parent_route`: within the rows of one device no device is named by more than 8 rows, and this bound is reached. `parent_slots`: the 64 entries of one device's coarse blocks are a permutation of 0 to 63.
All inputs are finite; a program needn't handle non-finite values.
Results may differ from the reference program's by a relative error of at most 0.013.
Values may be sent and summed in bfloat16 or wider, within the bound.
A program may use at most 64 MiB of HBM per device.

```python
import math
import jax
import jax.numpy as jnp
import numpy as np
from jax import lax

C_F = 96
C_C = 192
VOXELS = 512
FB_DEV = 32
CAP = 8
CB_DEV = 8
FINE_BLOCKS = 256
COARSE_BLOCKS = 64
N_SPACE = 8


def draw_parent_slots(key, part):
    key = jax.random.fold_in(key, 11)
    owners = COARSE_BLOCKS // CB_DEV
    per_source = CB_DEV * 8 // owners
    keys = jax.random.split(key, owners)

    def one_owner(single):
        first, second = jax.random.split(single)
        order = jax.random.permutation(first, owners).astype(jnp.int32)
        sequence = (order[:, None] * per_source + jnp.arange(per_source, dtype=jnp.int32)[None, :]).reshape(CB_DEV, 8)
        row_keys = jax.random.split(second, CB_DEV)
        return jax.vmap(lambda row_key, row: jax.random.permutation(row_key, row))(row_keys, sequence)
    rows = jax.vmap(one_owner)(keys)
    return rows.reshape(COARSE_BLOCKS, 8).astype(jnp.int32)


def levels(own_key, extent, cuts, smallest, high):
    level = 1.0
    for axis_at, parts in cuts:
        steps = jax.random.uniform(jax.random.fold_in(jax.random.fold_in(own_key, 6), axis_at), (parts,), jnp.float32, smallest / len(cuts), high / len(cuts))
        level = level * jnp.repeat(jnp.exp(steps), extent[axis_at] // parts).reshape((-1,) + (1,) * (len(extent) - 1 - axis_at))
    return level


def deal_out(rng, own, number, rows, count, top, bound, lean):
    ranking = jax.random.permutation(rng, count)
    packed, usual = shares(count, rows * top, bound, lean, True), shares(count, rows * top, bound, lean, False)
    places = jnp.arange(count)

    def named(tallies, rotation):
        used = int((tallies > 0).sum())
        fixed = max(1, used // 4)
        passed = fixed + (places - fixed + rotation * (used - fixed)) % max(1, count - fixed)
        return jnp.zeros((count,), jnp.int32).at[ranking[jnp.where(places < fixed, places, passed)]].set(jnp.asarray(tallies, jnp.int32))

    tallies = jnp.where(number % 4 == 0, named(packed, number // 4), named(usual, number - number // 4 - 1))
    mixed = jax.random.permutation(jax.random.fold_in(own, 3), count)
    giver, taker = mixed[0:count // 2 * 2:2], mixed[1:count // 2 * 2:2]
    margin = jnp.minimum(tallies[giver] - 1, bound - tallies[taker]) // 2
    margin = jnp.where((giver == ranking[0]) | (taker == ranking[0]) | (tallies[taker] == 0), 0, jnp.maximum(margin, 0))
    passed = jax.random.randint(jax.random.fold_in(own, 4), (count // 2,), 0, 1 << 20) % (margin + 1)
    tallies = tallies.at[giver].add(-passed).at[taker].add(passed)
    items = jnp.searchsorted(jnp.cumsum(tallies), jnp.arange(rows * top), side="right").astype(jnp.int32)
    grid = items.reshape(top, rows).T
    grid = grid[jax.random.permutation(jax.random.fold_in(own, 1), rows)]
    rotation = jax.random.randint(jax.random.fold_in(own, 2), (rows, 1), 0, top)
    return jnp.take_along_axis(grid, (jnp.arange(top)[None, :] + rotation) % top, axis=1)


def shares(count, total, bound, skew, full):
    loads = [(1 << 20) // math.isqrt(grade ** skew) + 1 for grade in range(1, count + 1)]
    largest = bound if full else min(bound, max(-(-total // count), total * loads[0] // sum(loads)))
    least = 1 if total - largest >= count - 1 else 0
    given, rest = [largest] + [least] * (count - 1), total - largest - least * (count - 1)
    while rest > 0:
        free = [i for i in range(1, count) if given[i] < largest] or [i for i in range(1, count) if given[i] < bound]
        pool, budget = sum([loads[i] for i in free]), rest
        for i in free:
            extra = min(bound - given[i], max(1, budget * loads[i] // pool), rest)
            given[i] = given[i] + extra
            rest = rest - extra
    return np.array(given)


def noise(key, shape, spread, reach, shards=(), kind=jnp.bfloat16):
    values = jax.random.normal(key, shape, jnp.float32) * spread
    if len(shards) > 0:
        values = levels(key, shape, shards, -0.22, 0.18) * values
    return jnp.clip(values, min=-reach, max=reach).astype(kind)


def setup_inputs(seed: int = 0) -> dict:
    key_list = jax.random.split(jax.random.key(seed), 8)
    fine_tiles = noise(key_list[0], (FINE_BLOCKS, C_F, VOXELS), 1.0, 6.0, ((0, 8), (1, 4)))
    parent_route_keys = jax.random.split(jax.random.fold_in(key_list[1], 1), FINE_BLOCKS // FB_DEV)
    parent_route_turns = jax.random.permutation(jax.random.fold_in(key_list[1], 3), FINE_BLOCKS // FB_DEV)
    parent_route = jax.vmap(lambda own, number: deal_out(jax.random.fold_in(key_list[1], 2), own, number, FB_DEV, N_SPACE, 1, CAP, 2))(parent_route_keys, parent_route_turns).reshape((FINE_BLOCKS, 1))
    parent_slots = draw_parent_slots(jax.random.fold_in(key_list[7], 71), 0)
    w_down = noise(key_list[3], (8, C_F, C_C), (8 * C_F) ** -0.5, 0.21875)
    coarse_bias = noise(key_list[4], (C_C,), 1.0, 4.0, (), jnp.float32)
    w_mid = noise(key_list[5], (C_C, C_C), C_C ** -0.5, 0.4375)
    w_up = noise(key_list[6], (8, C_C, C_F), C_C ** -0.5, 0.4375)
    return {"fine_tiles": fine_tiles, "parent_route": parent_route, "parent_slots": parent_slots, "w_down": w_down, "coarse_bias": coarse_bias, "w_mid": w_mid, "w_up": w_up}


def partner_octants(values):
    shaped = values.reshape(values.shape[0], 4, 2, values.shape[2], values.shape[3])
    return shaped[:, :, ::-1].reshape(values.shape)


def reference(fine_tiles, parent_route, parent_slots, w_down, coarse_bias, w_mid, w_up):
    devices_space = N_SPACE
    destinations = parent_route.reshape(devices_space, FB_DEV).astype(jnp.int32)
    matches = (destinations[:, :, None] == jnp.arange(devices_space, dtype=jnp.int32)[None, None, :]).astype(jnp.int32)
    within_rank = jnp.sum(matches * (jnp.cumsum(matches, axis=1) - 1), axis=2).astype(jnp.int32)
    source_ids = jnp.arange(devices_space, dtype=jnp.int32)[:, None]
    child_key = ((destinations * devices_space + source_ids) * CAP + within_rank).reshape(-1).astype(jnp.int32)
    owner_ids = (jnp.arange(COARSE_BLOCKS, dtype=jnp.int32) // CB_DEV)[:, None]
    parent_key = (owner_ids * (devices_space * CAP) + parent_slots.astype(jnp.int32)).reshape(-1).astype(jnp.int32)
    table_size = devices_space * devices_space * CAP
    child_table = jnp.full((table_size,), FINE_BLOCKS, jnp.int32).at[child_key].set(jnp.arange(FINE_BLOCKS, dtype=jnp.int32))
    child_of = child_table[parent_key].astype(jnp.int32)
    octant_table = jnp.zeros((table_size,), jnp.int32).at[parent_key].set(jnp.arange(COARSE_BLOCKS * 8, dtype=jnp.int32))
    octant_of = octant_table[child_key].astype(jnp.int32)
    padded = jnp.concatenate([fine_tiles, jnp.zeros((1, C_F, VOXELS), fine_tiles.dtype)], axis=0)
    down_f = w_down.astype(jnp.float32)
    mid_f = w_mid.astype(jnp.float32)
    up_f = w_up.astype(jnp.float32)

    def coarse_part(indices):
        children = padded[indices].reshape(CB_DEV, 8, C_F, 8, VOXELS // 8).astype(jnp.float32)
        coarse_pre = jnp.einsum('gqiop,oic->gqcp', children, down_f).astype(jnp.bfloat16)
        coarse_act = jax.nn.silu(coarse_pre.astype(jnp.float32) + coarse_bias[None, None, :, None]).astype(jnp.bfloat16)
        act_f = coarse_act.astype(jnp.float32)
        paired = act_f + partner_octants(act_f)
        return jnp.einsum('gqcp,ce->gqep', paired, mid_f).astype(jnp.bfloat16)

    coarse_out = lax.map(coarse_part, child_of.reshape(devices_space, CB_DEV * 8))
    flat_out = coarse_out.reshape(COARSE_BLOCKS * 8, C_C, VOXELS // 8)

    def fine_part(pair):
        blocks_here, where = pair
        octants = flat_out[where].astype(jnp.float32)
        lifted = jnp.einsum('jcp,ocf->jfop', octants, up_f).reshape(FB_DEV, C_F, VOXELS)
        return (blocks_here.astype(jnp.float32) + lifted).astype(jnp.bfloat16)

    result = lax.map(fine_part, (fine_tiles.reshape(devices_space, FB_DEV, C_F, VOXELS), octant_of.reshape(devices_space, FB_DEV)))
    return result.reshape(FINE_BLOCKS, C_F, VOXELS)
```

```python
import functools

import jax
import jax.numpy as jnp
from jax import lax
from jax.experimental import pallas as pl
from jax.experimental.pallas import tpu as pltpu
from jax.sharding import PartitionSpec as P

MESH = pl.DeviceIdType.MESH
LANES = 128
ROWS = 16
BF16 = jnp.bfloat16
F32 = jnp.float32


def route_kernel(capacity, route_ref, slots_ref, block_of, partner_of, slot_of, count):
    blocks = route_ref.shape[0]
    pairs = blocks // 2
    slot_count = block_of.shape[0]
    half = slot_count // 2

    def clear(t, carry):
        block_of[t] = 2 * pairs
        return carry

    lax.fori_loop(0, slot_count, clear, 0, unroll=8)

    def clear_count(d, carry):
        count[d] = 0
        return carry

    lax.fori_loop(0, count.shape[0], clear_count, 0, unroll=8)

    def place(j, carry):
        d = route_ref[j, 0]
        r = count[d]
        count[d] = r + 1
        slot = d * capacity + r
        block_of[slot] = (j % 2) * pairs + j // 2
        slot_of[j] = (slot % 2) * half + slot // 2
        return carry

    lax.fori_loop(0, blocks, place, 0, unroll=4)

    def pair(g, carry):
        for q in range(0, 8, 2):
            a = slots_ref[g, q]
            b = slots_ref[g, q + 1]
            partner_of[a] = (b % 2) * half + b // 2
            partner_of[b] = (a % 2) * half + a // 2
        return carry

    lax.fori_loop(0, slots_ref.shape[0], pair, 0, unroll=2)


def main_kernel(
    n, capacity, block_of, partner_of, slot_of, tiles, w_down, bias, w_mid, w_up, out,
    down_t, mid_t, up_t, bias_t, part, core_in, x_out, x_in, acts, going, arrived, twice,
    back, returned, again, full, core_s, core_r, x_s, x_r, go_s, go_r, back_s, back_r,
    share_s, share_r, all_s, all_r,
):
    blocks, fine_share, voxels = tiles.shape
    pairs = blocks // 2
    width = w_down.shape[2]
    chunks = part.shape[1]
    per_dest = capacity // 2
    half = n * per_dest
    me = lax.axis_index("space")
    rank = lax.axis_index("chan")
    hi, lo = rank // 2, rank % 2
    core_peer = 2 * hi + 1 - lo
    x_peer = 2 * (1 - hi) + lo

    barrier = pltpu.get_barrier_semaphore()

    def greet(off, carry):
        pl.semaphore_signal(
            barrier, inc=1, device_id=(lax.rem(me + off, n), rank), device_id_type=MESH
        )
        return carry

    lax.fori_loop(1, n, greet, 0)
    for peer in (core_peer, x_peer):
        pl.semaphore_signal(barrier, inc=1, device_id=(me, peer), device_id_type=MESH)

    left = lax.broadcasted_iota(jnp.int32, (1, LANES), 1) < LANES // 2

    def swap(v):
        return pltpu.roll(v, LANES // 2, 1)

    pad = 32
    row = lax.broadcasted_iota(jnp.int32, (pad, w_down.shape[1]), 0)
    col = lax.broadcasted_iota(jnp.int32, (pad, w_down.shape[1]), 1)
    pick = jnp.where((row < fine_share) & (col == rank * fine_share + row), 1.0, 0.0).astype(BF16)
    for parity in range(2):
        stacked = jnp.concatenate(
            [
                jnp.dot(pick, w_down[2 * a + parity], preferred_element_type=F32)
                for a in range(4)
            ],
            axis=0,
        )
        down_t[parity] = stacked.T.astype(BF16)

    zeros = jnp.zeros((pad - fine_share, LANES), F32)

    def down(step, carry):
        columns = []
        for b in range(4):
            tile = tiles[step * 4 + b].astype(F32)
            pieces = []
            for a in range(4):
                pieces += [tile[:, a * LANES : (a + 1) * LANES], zeros]
            columns.append(jnp.concatenate(pieces, axis=0).astype(BF16))
        x = jnp.concatenate(columns, axis=1)
        even = jnp.dot(down_t[0], x, preferred_element_type=F32)
        odd = jnp.dot(down_t[1], x, preferred_element_type=F32)
        for u in range(2):
            e0, e1 = even[:, 2 * u * LANES :][:, :LANES], even[:, (2 * u + 1) * LANES :][:, :LANES]
            o0, o1 = odd[:, 2 * u * LANES :][:, :LANES], odd[:, (2 * u + 1) * LANES :][:, :LANES]
            both = (jnp.where(left, e0, o1) + swap(jnp.where(left, e1, o0))).astype(BF16)
            for h in range(2):
                for l in range(2):
                    for ch in range(chunks):
                        at = (2 * h + l) * chunks * ROWS + ch * ROWS
                        part[l, ch, h, step * 2 + u] = both[at : at + ROWS]
        return carry

    lax.fori_loop(0, blocks // 4, down, 0)

    pl.semaphore_wait(barrier, n + 1)

    def to(src, dst, send, recv, space, chan):
        return pltpu.make_async_remote_copy(
            src_ref=src, dst_ref=dst, send_sem=send, recv_sem=recv,
            device_id=(space, chan), device_id_type=MESH,
        )

    cores = [
        to(part.at[1 - lo, ch], core_in.at[ch], core_s.at[ch], core_r.at[ch], me, core_peer)
        for ch in range(chunks)
    ]
    for copy in cores:
        copy.start()

    bias_t[...] = jnp.broadcast_to(bias[...], (LANES, width)).T.reshape(
        4 * chunks, ROWS, LANES
    )

    xs = [to(x_out.at[ch], x_in.at[ch], x_s.at[ch], x_r.at[ch], me, x_peer) for ch in range(chunks)]
    for ch in range(chunks):
        cores[ch].wait_recv()
        x_out[ch] = (
            part[lo, ch, 1 - hi].astype(F32) + core_in[ch, 1 - hi].astype(F32)
        ).astype(BF16)
        xs[ch].start()

    def silu(v):
        return v / (1.0 + jnp.exp(-v))

    def spread(ref, ch, flat, count):
        swapped = swap(flat)
        ref[ch, 0:count] = jnp.where(left, flat, swapped).astype(BF16).reshape(count, ROWS, LANES)
        ref[ch, count : 2 * count] = (
            jnp.where(left, swapped, flat).astype(BF16).reshape(count, ROWS, LANES)
        )

    def joined(ref, ch, first, second):
        return jnp.where(left, ref[ch, first].astype(F32), ref[ch, second].astype(F32))

    def exchange(src, dst, send, recv, ch, d):
        return to(src.at[ch, d], dst.at[ch, me], send.at[ch], recv.at[ch], d, rank)

    other = lax.rem(me + 1, n)

    def whole(src, dst, send, recv, ch):
        return to(
            src.at[ch, pl.ds(0, n - 1)], dst.at[ch, pl.ds(0, n - 1)], send.at[ch], recv.at[ch],
            other, rank,
        )

    for ch in range(chunks):
        xs[ch].wait_recv()
        b = bias_t[rank * chunks + ch]
        total = (
            part[lo, ch, hi].astype(F32)
            + core_in[ch, hi].astype(F32)
            + x_in[ch].astype(F32)
            + b[None]
        )
        spread(acts, ch, silu(total).reshape(pairs * ROWS, LANES), pairs)
        acts[ch, 2 * pairs] = silu(b).astype(BF16)

        def send(off, carry, ch=ch):
            d = lax.rem(me + off, n)
            for m in range(per_dest):
                t = d * capacity + 2 * m
                going[ch, d, m] = joined(acts, ch, block_of[t], block_of[t + 1]).astype(BF16)
            exchange(going, arrived, go_s, go_r, ch, d).start()
            return carry

        lax.fori_loop(1, n, send, 0)
        for m in range(per_dest):
            t = me * capacity + 2 * m
            arrived[ch, me, m] = joined(acts, ch, block_of[t], block_of[t + 1]).astype(BF16)

    row = lax.broadcasted_iota(jnp.int32, (fine_share, w_up.shape[2]), 0)
    col = lax.broadcasted_iota(jnp.int32, (fine_share, w_up.shape[2]), 1)
    pick_up = jnp.where(col == rank * fine_share + row, 1.0, 0.0).astype(BF16)
    up_t[...] = jnp.concatenate(
        [
            lax.dot_general(
                pick_up, w_up[o], (((1,), (1,)), ((), ())), preferred_element_type=F32
            )
            for o in range(8)
        ],
        axis=0,
    ).astype(BF16)
    mid = w_mid[...].astype(F32)
    ordered = []
    for l in range(2):
        for ch in range(chunks):
            for h in range(2):
                at = (2 * h + l) * chunks * ROWS + ch * ROWS
                ordered.append(mid[at : at + ROWS])
    mid_t[...] = jnp.concatenate(ordered, axis=0).T.astype(BF16)

    for ch in range(chunks):
        whole(going, arrived, go_s, go_r, ch).wait_recv()
        spread(
            twice, ch, arrived[ch].astype(F32).reshape(half * ROWS, LANES), half
        )

        def paired(d, ch=ch):
            sums = []
            for m in range(per_dest):
                t = d * capacity + 2 * m
                own = arrived[ch, d, m].astype(F32)
                sums.append(
                    (own + joined(twice, ch, partner_of[t], partner_of[t + 1])).astype(BF16)
                )
            return sums

        def send_back(off, carry, ch=ch, paired=paired):
            d = lax.rem(me + off, n)
            for m, value in enumerate(paired(d)):
                back[ch, d, m] = value
            exchange(back, returned, back_s, back_r, ch, d).start()
            return carry

        lax.fori_loop(1, n, send_back, 0)
        for m, value in enumerate(paired(me)):
            returned[ch, me, m] = value

    shares = [
        to(full.at[lo, ch, hi], full.at[lo, ch, hi], share_s.at[ch], share_r.at[ch], me, x_peer)
        for ch in range(chunks)
    ]
    alls = [
        to(full.at[lo, ch], full.at[lo, ch], all_s.at[ch], all_r.at[ch], me, core_peer)
        for ch in range(chunks)
    ]
    for ch in range(chunks):
        whole(back, returned, back_s, back_r, ch).wait_recv()
        spread(
            again, ch, returned[ch].astype(F32).reshape(half * ROWS, LANES), half
        )

        def collect(m, carry, ch=ch):
            full[lo, ch, hi, m] = joined(again, ch, slot_of[2 * m], slot_of[2 * m + 1]).astype(BF16)
            return carry

        lax.fori_loop(0, pairs, collect, 0, unroll=4)
        shares[ch].start()
    for ch in range(chunks):
        shares[ch].wait_recv()
        alls[ch].start()
    for ch in range(chunks):
        alls[ch].wait_recv()

    def up(step, carry):
        x = jnp.concatenate(
            [full[:, :, :, step * 2 + u].reshape(width, LANES) for u in range(2)], axis=1
        )
        coarse = jnp.dot(mid_t[...], x, preferred_element_type=F32).astype(BF16)
        lifted = jnp.dot(up_t[...], coarse, preferred_element_type=F32)
        for u in range(2):
            mine = lifted[:, u * LANES : (u + 1) * LANES]
            swapped = swap(mine)
            for b in range(2):
                j = step * 4 + 2 * u + b
                first, second = (mine, swapped) if b == 0 else (swapped, mine)
                for a in range(4):
                    r0, r1 = 2 * a * fine_share, (2 * a + 1) * fine_share
                    value = jnp.where(
                        left, first[r0 : r0 + fine_share], second[r1 : r1 + fine_share]
                    )
                    at = pl.ds(a * LANES, LANES)
                    out[j, :, at] = (tiles[j, :, at].astype(F32) + value).astype(BF16)
        return carry

    lax.fori_loop(0, pairs // 2, up, 0)

    for ch in range(chunks):
        cores[ch].wait_send()
        xs[ch].wait_send()
        whole(going, arrived, go_s, go_r, ch).wait_send()
        whole(back, returned, back_s, back_r, ch).wait_send()
        shares[ch].wait_send()
        alls[ch].wait_send()


def local(fine_tiles, parent_route, parent_slots, w_down, coarse_bias, w_mid, w_up):
    n = lax.axis_size("space")
    blocks = fine_tiles.shape[0]
    pairs = blocks // 2
    width = w_down.shape[2]
    slot_count = parent_slots.shape[0] * 8
    capacity = slot_count // n
    per_dest = capacity // 2
    half = slot_count // 2
    chunks = width // (4 * ROWS)
    smem = pl.BlockSpec(memory_space=pltpu.SMEM)
    vmem = pl.BlockSpec(memory_space=pltpu.VMEM)
    ints = jax.ShapeDtypeStruct((slot_count,), jnp.int32)
    tables = pl.pallas_call(
        functools.partial(route_kernel, capacity),
        out_shape=(ints, ints, jax.ShapeDtypeStruct((blocks,), jnp.int32)),
        in_specs=[smem, smem],
        out_specs=(smem, smem, smem),
        scratch_shapes=[pltpu.SMEM((n,), jnp.int32)],
    )(parent_route, parent_slots)

    def buffer(*shape):
        return pltpu.VMEM(shape + (ROWS, LANES), BF16)

    return pl.pallas_call(
        functools.partial(main_kernel, n, capacity),
        out_shape=jax.ShapeDtypeStruct(fine_tiles.shape, fine_tiles.dtype),
        in_specs=[smem] * 3 + [vmem] * 5,
        out_specs=vmem,
        scratch_shapes=[
            pltpu.VMEM((2, width, LANES), BF16),
            pltpu.VMEM((width, width), BF16),
            pltpu.VMEM((8 * fine_tiles.shape[1], width), BF16),
            pltpu.VMEM((4 * chunks, ROWS, LANES), F32),
            buffer(2, chunks, 2, pairs),
            buffer(chunks, 2, pairs),
            buffer(chunks, pairs),
            buffer(chunks, pairs),
            buffer(chunks, 2 * pairs + 1),
            buffer(chunks, n, per_dest),
            buffer(chunks, n, per_dest),
            buffer(chunks, 2 * half),
            buffer(chunks, n, per_dest),
            buffer(chunks, n, per_dest),
            buffer(chunks, 2 * half),
            buffer(2, chunks, 2, pairs),
        ]
        + [pltpu.SemaphoreType.DMA((chunks,))] * 12,
        compiler_params=pltpu.CompilerParams(
            collective_id=0, has_side_effects=True, vmem_limit_bytes=32 * 1024 * 1024
        ),
    )(*tables, fine_tiles, w_down, coarse_bias.reshape(1, width), w_mid, w_up)


def solution(mesh):
    in_specs = (P("space", "chan", None), P("space", None), P("space", None), P(), P(), P(), P())
    out_specs = P("space", "chan", None)
    return jax.shard_map(local, mesh=mesh, in_specs=in_specs, out_specs=out_specs, check_vma=False)
```

```python
import functools

import jax
import jax.numpy as jnp
from jax import lax
from jax.experimental import pallas as pl
from jax.experimental.pallas import tpu as pltpu
from jax.sharding import PartitionSpec as P

MESH = pl.DeviceIdType.MESH
LANES = 128
ROWS = 16
BF16 = jnp.bfloat16
F32 = jnp.float32


def build_tables(n, capacity, route, slots, tables):
    blocks = route.shape[1]
    pairs = blocks // 2
    half = n * capacity // 2
    lanes = tables.shape[1]

    def place(slot):
        return (slot % 2) * half + slot // 2

    j_row = lax.broadcasted_iota(jnp.int32, (blocks, blocks), 0)
    j_col = lax.broadcasted_iota(jnp.int32, (blocks, blocks), 1)
    row = jnp.broadcast_to(route[...], (blocks, blocks))
    own = jnp.sum(jnp.where(j_row == j_col, row, 0), axis=1, keepdims=True)
    earlier = jnp.where((row == own) & (j_col < j_row), 1, 0)
    slot = own * capacity + jnp.sum(earlier, axis=1, keepdims=True)
    j = lax.broadcasted_iota(jnp.int32, (blocks, lanes), 0)
    t = lax.broadcasted_iota(jnp.int32, (blocks, lanes), 1)
    named = jnp.where(slot == t, (j % 2) * pairs + j // 2 - 2 * pairs, 0)
    tables[...] = jnp.zeros_like(tables)
    tables[0:1] = jnp.sum(named, axis=0, keepdims=True) + 2 * pairs
    tables[2:3] = jnp.sum(jnp.where(j == t, place(slot), 0), axis=0, keepdims=True)
    t = lax.broadcasted_iota(jnp.int32, (slots.shape[0], lanes), 1)
    partner = jnp.zeros((slots.shape[0], lanes), jnp.int32)
    for q in range(8):
        mate = q + 1 - 2 * (q % 2)
        partner += jnp.where(slots[:, q : q + 1] == t, place(slots[:, mate : mate + 1]), 0)
    tables[1:2] = jnp.sum(partner, axis=0, keepdims=True)


def main_kernel(
    n, capacity, route_in, slots_in, tiles_in, down_in, bias_in, mid_in, up_in, out,
    tiles, w_down, bias, w_mid, w_up, route, slots, tables, index, load_s, store_s, table_s,
    down_t, mid_t, up_t, bias_t, part, core_in, x_out, x_in, acts, going, arrived, twice,
    back, returned, again, full, core_s, core_r, x_s, x_r, go_s, go_r, back_s, back_r,
    share_s, share_r, all_s, all_r,
):
    blocks, fine_share, voxels = tiles.shape
    pieces_in = 4
    piece = blocks // pieces_in
    sources = [(down_in, w_down), (route_in, route), (slots_in, slots)]
    for p in range(pieces_in):
        at = pl.ds(p * piece, piece)
        sources.append((tiles_in.at[at], tiles.at[at]))
    sources += [(bias_in, bias), (mid_in, w_mid), (up_in, w_up)]
    loads = [
        pltpu.make_async_copy(src, dst, load_s.at[i]) for i, (src, dst) in enumerate(sources)
    ]
    for load in loads:
        load.start()
    pairs = blocks // 2
    width = w_down.shape[2]
    chunks = part.shape[1]
    per_dest = capacity // 2
    half = n * per_dest
    me = lax.axis_index("space")
    rank = lax.axis_index("chan")
    hi, lo = rank // 2, rank % 2
    core_peer = 2 * hi + 1 - lo
    x_peer = 2 * (1 - hi) + lo

    barrier = pltpu.get_barrier_semaphore()

    def greet(off, carry):
        pl.semaphore_signal(
            barrier, inc=1, device_id=(lax.rem(me + off, n), rank), device_id_type=MESH
        )
        return carry

    lax.fori_loop(1, n, greet, 0)
    for peer in (core_peer, x_peer):
        pl.semaphore_signal(barrier, inc=1, device_id=(me, peer), device_id_type=MESH)

    left = lax.broadcasted_iota(jnp.int32, (1, LANES), 1) < LANES // 2

    def swap(v):
        return pltpu.roll(v, LANES // 2, 1)

    pad = 32
    row = lax.broadcasted_iota(jnp.int32, (pad, w_down.shape[1]), 0)
    col = lax.broadcasted_iota(jnp.int32, (pad, w_down.shape[1]), 1)
    loads[1].wait()
    loads[2].wait()
    build_tables(n, capacity, route, slots, tables)
    table_copy = pltpu.make_async_copy(tables, index, table_s)
    table_copy.start()
    loads[0].wait()
    pick = jnp.where((row < fine_share) & (col == rank * fine_share + row), 1.0, 0.0).astype(BF16)
    for parity in range(2):
        stacked = jnp.concatenate(
            [
                jnp.dot(pick, w_down[2 * a + parity], preferred_element_type=F32)
                for a in range(4)
            ],
            axis=0,
        )
        down_t[parity] = stacked.T.astype(BF16)

    zeros = jnp.zeros((pad - fine_share, LANES), F32)

    def down(step, carry):
        columns = []
        for b in range(4):
            tile = tiles[step * 4 + b].astype(F32)
            pieces = []
            for a in range(4):
                pieces += [tile[:, a * LANES : (a + 1) * LANES], zeros]
            columns.append(jnp.concatenate(pieces, axis=0).astype(BF16))
        x = jnp.concatenate(columns, axis=1)
        even = jnp.dot(down_t[0], x, preferred_element_type=F32)
        odd = jnp.dot(down_t[1], x, preferred_element_type=F32)
        for u in range(2):
            e0, e1 = even[:, 2 * u * LANES :][:, :LANES], even[:, (2 * u + 1) * LANES :][:, :LANES]
            o0, o1 = odd[:, 2 * u * LANES :][:, :LANES], odd[:, (2 * u + 1) * LANES :][:, :LANES]
            both = (jnp.where(left, e0, o1) + swap(jnp.where(left, e1, o0))).astype(BF16)
            for h in range(2):
                for l in range(2):
                    for ch in range(chunks):
                        at = (2 * h + l) * chunks * ROWS + ch * ROWS
                        part[l, ch, h, step * 2 + u] = both[at : at + ROWS]
        return carry

    for p in range(pieces_in):
        loads[3 + p].wait()
        lax.fori_loop(p * piece // 4, (p + 1) * piece // 4, down, 0)

    pl.semaphore_wait(barrier, n + 1)

    def to(src, dst, send, recv, space, chan):
        return pltpu.make_async_remote_copy(
            src_ref=src, dst_ref=dst, send_sem=send, recv_sem=recv,
            device_id=(space, chan), device_id_type=MESH,
        )

    cores = [
        to(part.at[1 - lo, ch], core_in.at[ch], core_s.at[ch], core_r.at[ch], me, core_peer)
        for ch in range(chunks)
    ]
    for copy in cores:
        copy.start()

    loads[3 + pieces_in].wait()
    bias_t[...] = jnp.broadcast_to(bias[...], (LANES, width)).T.reshape(
        4 * chunks, ROWS, LANES
    )

    xs = [to(x_out.at[ch], x_in.at[ch], x_s.at[ch], x_r.at[ch], me, x_peer) for ch in range(chunks)]
    for ch in range(chunks):
        cores[ch].wait_recv()
        x_out[ch] = (
            part[lo, ch, 1 - hi].astype(F32) + core_in[ch, 1 - hi].astype(F32)
        ).astype(BF16)
        xs[ch].start()

    def silu(v):
        return v / (1.0 + jnp.exp(-v))

    def spread(ref, ch, flat, count):
        swapped = swap(flat)
        ref[ch, 0:count] = jnp.where(left, flat, swapped).astype(BF16).reshape(count, ROWS, LANES)
        ref[ch, count : 2 * count] = (
            jnp.where(left, swapped, flat).astype(BF16).reshape(count, ROWS, LANES)
        )

    def joined(ref, ch, first, second):
        return jnp.where(left, ref[ch, first].astype(F32), ref[ch, second].astype(F32))

    def exchange(src, dst, send, recv, ch, d):
        return to(src.at[ch, d], dst.at[ch, me], send.at[ch], recv.at[ch], d, rank)

    other = lax.rem(me + 1, n)

    def whole(src, dst, send, recv, ch):
        return to(
            src.at[ch, pl.ds(0, n - 1)], dst.at[ch, pl.ds(0, n - 1)], send.at[ch], recv.at[ch],
            other, rank,
        )

    table_copy.wait()
    for ch in range(chunks):
        xs[ch].wait_recv()
        b = bias_t[rank * chunks + ch]
        total = (
            part[lo, ch, hi].astype(F32)
            + core_in[ch, hi].astype(F32)
            + x_in[ch].astype(F32)
            + b[None]
        )
        spread(acts, ch, silu(total).reshape(pairs * ROWS, LANES), pairs)
        acts[ch, 2 * pairs] = silu(b).astype(BF16)

        def send(off, carry, ch=ch):
            d = lax.rem(me + off, n)
            for m in range(per_dest):
                t = d * capacity + 2 * m
                going[ch, d, m] = joined(acts, ch, index[0, t], index[0, t + 1]).astype(BF16)
            exchange(going, arrived, go_s, go_r, ch, d).start()
            return carry

        lax.fori_loop(1, n, send, 0)
        for m in range(per_dest):
            t = me * capacity + 2 * m
            arrived[ch, me, m] = joined(acts, ch, index[0, t], index[0, t + 1]).astype(BF16)

    loads[4 + pieces_in].wait()
    loads[5 + pieces_in].wait()
    row = lax.broadcasted_iota(jnp.int32, (fine_share, w_up.shape[2]), 0)
    col = lax.broadcasted_iota(jnp.int32, (fine_share, w_up.shape[2]), 1)
    pick_up = jnp.where(col == rank * fine_share + row, 1.0, 0.0).astype(BF16)
    up_t[...] = jnp.concatenate(
        [
            lax.dot_general(
                pick_up, w_up[o], (((1,), (1,)), ((), ())), preferred_element_type=F32
            )
            for o in range(8)
        ],
        axis=0,
    ).astype(BF16)
    mid = w_mid[...].astype(F32)
    ordered = []
    for l in range(2):
        for ch in range(chunks):
            for h in range(2):
                at = (2 * h + l) * chunks * ROWS + ch * ROWS
                ordered.append(mid[at : at + ROWS])
    mid_t[...] = jnp.concatenate(ordered, axis=0).T.astype(BF16)

    for ch in range(chunks):
        whole(going, arrived, go_s, go_r, ch).wait_recv()
        spread(
            twice, ch, arrived[ch].astype(F32).reshape(half * ROWS, LANES), half
        )

        def paired(d, ch=ch):
            sums = []
            for m in range(per_dest):
                t = d * capacity + 2 * m
                own = arrived[ch, d, m].astype(F32)
                sums.append(
                    (own + joined(twice, ch, index[1, t], index[1, t + 1])).astype(BF16)
                )
            return sums

        def send_back(off, carry, ch=ch, paired=paired):
            d = lax.rem(me + off, n)
            for m, value in enumerate(paired(d)):
                back[ch, d, m] = value
            exchange(back, returned, back_s, back_r, ch, d).start()
            return carry

        lax.fori_loop(1, n, send_back, 0)
        for m, value in enumerate(paired(me)):
            returned[ch, me, m] = value

    shares = [
        to(full.at[lo, ch, hi], full.at[lo, ch, hi], share_s.at[ch], share_r.at[ch], me, x_peer)
        for ch in range(chunks)
    ]
    alls = [
        to(full.at[lo, ch], full.at[lo, ch], all_s.at[ch], all_r.at[ch], me, core_peer)
        for ch in range(chunks)
    ]
    for ch in range(chunks):
        whole(back, returned, back_s, back_r, ch).wait_recv()
        spread(
            again, ch, returned[ch].astype(F32).reshape(half * ROWS, LANES), half
        )

        def collect(m, carry, ch=ch):
            full[lo, ch, hi, m] = joined(again, ch, index[2, 2 * m], index[2, 2 * m + 1]).astype(BF16)
            return carry

        lax.fori_loop(0, pairs, collect, 0, unroll=4)
        shares[ch].start()
    for ch in range(chunks):
        shares[ch].wait_recv()
        alls[ch].start()
    for ch in range(chunks):
        alls[ch].wait_recv()

    def up(step, carry):
        x = jnp.concatenate(
            [full[:, :, :, step * 2 + u].reshape(width, LANES) for u in range(2)], axis=1
        )
        coarse = jnp.dot(mid_t[...], x, preferred_element_type=F32).astype(BF16)
        lifted = jnp.dot(up_t[...], coarse, preferred_element_type=F32)
        for u in range(2):
            mine = lifted[:, u * LANES : (u + 1) * LANES]
            swapped = swap(mine)
            for b in range(2):
                j = step * 4 + 2 * u + b
                first, second = (mine, swapped) if b == 0 else (swapped, mine)
                for a in range(4):
                    r0, r1 = 2 * a * fine_share, (2 * a + 1) * fine_share
                    value = jnp.where(
                        left, first[r0 : r0 + fine_share], second[r1 : r1 + fine_share]
                    )
                    at = pl.ds(a * LANES, LANES)
                    tiles[j, :, at] = (tiles[j, :, at].astype(F32) + value).astype(BF16)
        return carry

    stores = []
    for p in range(pieces_in):
        lax.fori_loop(p * piece // 4, (p + 1) * piece // 4, up, 0)
        at = pl.ds(p * piece, piece)
        stores.append(pltpu.make_async_copy(tiles.at[at], out.at[at], store_s.at[p]))
        stores[p].start()

    for ch in range(chunks):
        cores[ch].wait_send()
        xs[ch].wait_send()
        whole(going, arrived, go_s, go_r, ch).wait_send()
        whole(back, returned, back_s, back_r, ch).wait_send()
        shares[ch].wait_send()
        alls[ch].wait_send()
    for store in stores:
        store.wait()


def local(fine_tiles, parent_route, parent_slots, w_down, coarse_bias, w_mid, w_up):
    n = lax.axis_size("space")
    blocks = fine_tiles.shape[0]
    pairs = blocks // 2
    width = w_down.shape[2]
    slot_count = parent_slots.shape[0] * 8
    capacity = slot_count // n
    per_dest = capacity // 2
    half = slot_count // 2
    chunks = width // (4 * ROWS)
    hbm = pl.BlockSpec(memory_space=pltpu.HBM)
    lanes = -(-max(slot_count, blocks) // LANES) * LANES

    def buffer(*shape):
        return pltpu.VMEM(shape + (ROWS, LANES), BF16)

    return pl.pallas_call(
        functools.partial(main_kernel, n, capacity),
        out_shape=jax.ShapeDtypeStruct(fine_tiles.shape, fine_tiles.dtype),
        in_specs=[hbm] * 7,
        out_specs=hbm,
        scratch_shapes=[
            pltpu.VMEM(fine_tiles.shape, BF16),
            pltpu.VMEM(w_down.shape, BF16),
            pltpu.VMEM((1, width), F32),
            pltpu.VMEM(w_mid.shape, BF16),
            pltpu.VMEM(w_up.shape, BF16),
            pltpu.VMEM((1, blocks), jnp.int32),
            pltpu.VMEM(parent_slots.shape, jnp.int32),
            pltpu.VMEM((8, lanes), jnp.int32),
            pltpu.SMEM((8, lanes), jnp.int32),
            pltpu.SemaphoreType.DMA((10,)),
            pltpu.SemaphoreType.DMA((4,)),
            pltpu.SemaphoreType.DMA,
            pltpu.VMEM((2, width, LANES), BF16),
            pltpu.VMEM((width, width), BF16),
            pltpu.VMEM((8 * fine_tiles.shape[1], width), BF16),
            pltpu.VMEM((4 * chunks, ROWS, LANES), F32),
            buffer(2, chunks, 2, pairs),
            buffer(chunks, 2, pairs),
            buffer(chunks, pairs),
            buffer(chunks, pairs),
            buffer(chunks, 2 * pairs + 1),
            buffer(chunks, n, per_dest),
            buffer(chunks, n, per_dest),
            buffer(chunks, 2 * half),
            buffer(chunks, n, per_dest),
            buffer(chunks, n, per_dest),
            buffer(chunks, 2 * half),
            buffer(2, chunks, 2, pairs),
        ]
        + [pltpu.SemaphoreType.DMA((chunks,))] * 12,
        compiler_params=pltpu.CompilerParams(
            collective_id=0, has_side_effects=True, vmem_limit_bytes=62 * 1024 * 1024
        ),
    )(
        parent_route.reshape(1, blocks),
        parent_slots,
        fine_tiles,
        w_down,
        coarse_bias.reshape(1, width),
        w_mid,
        w_up,
    )


def solution(mesh):
    in_specs = (P("space", "chan", None), P("space", None), P("space", None), P(), P(), P(), P())
    out_specs = P("space", "chan", None)
    return jax.shard_map(local, mesh=mesh, in_specs=in_specs, out_specs=out_specs, check_vma=False)
```

```python
import functools

import jax
import jax.numpy as jnp
from jax import lax
from jax.experimental import pallas as pl
from jax.experimental.pallas import tpu as pltpu
from jax.sharding import PartitionSpec as P

MESH = pl.DeviceIdType.MESH
LANES = 128
ROWS = 16
BF16 = jnp.bfloat16
F32 = jnp.float32


def build_tables(n, capacity, route, slots, tables):
    blocks = route.shape[1]
    pairs = blocks // 2
    half = n * capacity // 2
    lanes = tables.shape[1]

    def place(slot):
        return (slot % 2) * half + slot // 2

    j_row = lax.broadcasted_iota(jnp.int32, (blocks, blocks), 0)
    j_col = lax.broadcasted_iota(jnp.int32, (blocks, blocks), 1)
    row = jnp.broadcast_to(route[...], (blocks, blocks))
    own = jnp.sum(jnp.where(j_row == j_col, row, 0), axis=1, keepdims=True)
    earlier = jnp.where((row == own) & (j_col < j_row), 1, 0)
    slot = own * capacity + jnp.sum(earlier, axis=1, keepdims=True)
    j = lax.broadcasted_iota(jnp.int32, (blocks, lanes), 0)
    t = lax.broadcasted_iota(jnp.int32, (blocks, lanes), 1)
    named = jnp.where(slot == t, (j % 2) * pairs + j // 2 - 2 * pairs, 0)
    tables[...] = jnp.zeros_like(tables)
    tables[0:1] = jnp.sum(named, axis=0, keepdims=True) + 2 * pairs
    tables[2:3] = jnp.sum(jnp.where(j == t, place(slot), 0), axis=0, keepdims=True)
    t = lax.broadcasted_iota(jnp.int32, (slots.shape[0], lanes), 1)
    partner = jnp.zeros((slots.shape[0], lanes), jnp.int32)
    for q in range(8):
        mate = q + 1 - 2 * (q % 2)
        partner += jnp.where(slots[:, q : q + 1] == t, place(slots[:, mate : mate + 1]), 0)
    tables[1:2] = jnp.sum(partner, axis=0, keepdims=True)


def main_kernel(
    n, capacity, route_in, slots_in, tiles_in, down_in, bias_in, mid_in, up_in, out,
    tiles, w_down, bias, w_mid, w_up, route, slots, tables, index, load_s, store_s, table_s,
    down_t, mid_t, up_t, bias_t, part, core_in, x_out, x_in, acts, going, arrived, twice,
    back, returned, again, full, core_s, core_r, x_s, x_r, go_s, go_r, back_s, back_r,
    share_s, share_r, all_s, all_r,
):
    blocks, fine_share, voxels = tiles.shape
    pieces_in = 4
    piece = blocks // pieces_in
    sources = [(down_in, w_down), (route_in, route), (slots_in, slots)]
    for p in range(pieces_in):
        at = pl.ds(p * piece, piece)
        sources.append((tiles_in.at[at], tiles.at[at]))
    sources += [(bias_in, bias), (mid_in, w_mid), (up_in, w_up)]
    loads = [
        pltpu.make_async_copy(src, dst, load_s.at[i]) for i, (src, dst) in enumerate(sources)
    ]
    for load in loads:
        load.start()
    pairs = blocks // 2
    width = w_down.shape[2]
    chunks = part.shape[1]
    per_dest = capacity // 2
    half = n * per_dest
    me = lax.axis_index("space")
    rank = lax.axis_index("chan")
    hi, lo = rank // 2, rank % 2
    core_peer = 2 * hi + 1 - lo
    x_peer = 2 * (1 - hi) + lo

    barrier = pltpu.get_barrier_semaphore()

    def greet(off, carry):
        pl.semaphore_signal(
            barrier, inc=1, device_id=(lax.rem(me + off, n), rank), device_id_type=MESH
        )
        return carry

    lax.fori_loop(1, n, greet, 0)
    for peer in (core_peer, x_peer):
        pl.semaphore_signal(barrier, inc=1, device_id=(me, peer), device_id_type=MESH)

    left = lax.broadcasted_iota(jnp.int32, (1, LANES), 1) < LANES // 2

    def swap(v):
        return pltpu.roll(v, LANES // 2, 1)

    pad = 32
    row = lax.broadcasted_iota(jnp.int32, (pad, w_down.shape[1]), 0)
    col = lax.broadcasted_iota(jnp.int32, (pad, w_down.shape[1]), 1)
    loads[1].wait()
    loads[2].wait()
    build_tables(n, capacity, route, slots, tables)
    table_copy = pltpu.make_async_copy(tables, index, table_s)
    table_copy.start()
    loads[0].wait()
    pick = jnp.where((row < fine_share) & (col == rank * fine_share + row), 1.0, 0.0).astype(BF16)
    for parity in range(2):
        stacked = jnp.concatenate(
            [
                jnp.dot(pick, w_down[2 * a + parity], preferred_element_type=F32)
                for a in range(4)
            ],
            axis=0,
        )
        down_t[parity] = stacked.T.astype(BF16)

    zeros = jnp.zeros((pad - fine_share, LANES), F32)

    def down(step, carry):
        columns = []
        for b in range(4):
            tile = tiles[step * 4 + b].astype(F32)
            pieces = []
            for a in range(4):
                pieces += [tile[:, a * LANES : (a + 1) * LANES], zeros]
            columns.append(jnp.concatenate(pieces, axis=0).astype(BF16))
        x = jnp.concatenate(columns, axis=1)
        even = jnp.dot(down_t[0], x, preferred_element_type=F32)
        odd = jnp.dot(down_t[1], x, preferred_element_type=F32)
        for u in range(2):
            e0, e1 = even[:, 2 * u * LANES :][:, :LANES], even[:, (2 * u + 1) * LANES :][:, :LANES]
            o0, o1 = odd[:, 2 * u * LANES :][:, :LANES], odd[:, (2 * u + 1) * LANES :][:, :LANES]
            both = (jnp.where(left, e0, o1) + swap(jnp.where(left, e1, o0))).astype(BF16)
            for h in range(2):
                for l in range(2):
                    for ch in range(chunks):
                        at = (2 * h + l) * chunks * ROWS + ch * ROWS
                        part[l, ch, h, step * 2 + u] = both[at : at + ROWS]
        return carry

    for p in range(pieces_in):
        loads[3 + p].wait()
        lax.fori_loop(p * piece // 4, (p + 1) * piece // 4, down, 0, unroll=2)

    pl.semaphore_wait(barrier, n + 1)

    def to(src, dst, send, recv, space, chan):
        return pltpu.make_async_remote_copy(
            src_ref=src, dst_ref=dst, send_sem=send, recv_sem=recv,
            device_id=(space, chan), device_id_type=MESH,
        )

    cores = [
        to(part.at[1 - lo, ch], core_in.at[ch], core_s.at[ch], core_r.at[ch], me, core_peer)
        for ch in range(chunks)
    ]
    for copy in cores:
        copy.start()

    loads[3 + pieces_in].wait()
    bias_t[...] = jnp.broadcast_to(bias[...], (LANES, width)).T.reshape(
        4 * chunks, ROWS, LANES
    )

    xs = [to(x_out.at[ch], x_in.at[ch], x_s.at[ch], x_r.at[ch], me, x_peer) for ch in range(chunks)]
    for ch in range(chunks):
        cores[ch].wait_recv()
        x_out[ch] = (
            part[lo, ch, 1 - hi].astype(F32) + core_in[ch, 1 - hi].astype(F32)
        ).astype(BF16)
        xs[ch].start()

    def silu(v):
        return v / (1.0 + jnp.exp(-v))

    def spread(ref, ch, flat, count):
        swapped = swap(flat)
        ref[ch, 0:count] = jnp.where(left, flat, swapped).astype(BF16).reshape(count, ROWS, LANES)
        ref[ch, count : 2 * count] = (
            jnp.where(left, swapped, flat).astype(BF16).reshape(count, ROWS, LANES)
        )

    def joined(ref, ch, first, second):
        return jnp.where(left, ref[ch, first].astype(F32), ref[ch, second].astype(F32))

    def mate(step):
        off = n - step
        if n & (n - 1):
            return lax.rem(me + off, n)
        d, bit = me, 1
        while bit < n:
            d = d + (off // bit) % 2 * (1 - 2 * ((me // bit) % 2)) * bit
            bit *= 2
        return d

    def exchange(src, dst, send, recv, ch, d):
        return to(src.at[ch, d], dst.at[ch, me], send.at[ch], recv.at[ch], d, rank)

    other = lax.rem(me + 1, n)

    def whole(src, dst, send, recv, ch):
        return to(
            src.at[ch, pl.ds(0, n - 1)], dst.at[ch, pl.ds(0, n - 1)], send.at[ch], recv.at[ch],
            other, rank,
        )

    table_copy.wait()
    for ch in range(chunks):
        xs[ch].wait_recv()
        b = bias_t[rank * chunks + ch]
        total = (
            part[lo, ch, hi].astype(F32)
            + core_in[ch, hi].astype(F32)
            + x_in[ch].astype(F32)
            + b[None]
        )
        spread(acts, ch, silu(total).reshape(pairs * ROWS, LANES), pairs)
        acts[ch, 2 * pairs] = silu(b).astype(BF16)

        def send(off, carry, ch=ch):
            d = mate(off)
            for m in range(per_dest):
                t = d * capacity + 2 * m
                going[ch, d, m] = joined(acts, ch, index[0, t], index[0, t + 1]).astype(BF16)
            exchange(going, arrived, go_s, go_r, ch, d).start()
            return carry

        lax.fori_loop(1, n, send, 0, unroll=n - 1 if n <= 8 else 1)
        for m in range(per_dest):
            t = me * capacity + 2 * m
            arrived[ch, me, m] = joined(acts, ch, index[0, t], index[0, t + 1]).astype(BF16)

    loads[4 + pieces_in].wait()
    loads[5 + pieces_in].wait()
    row = lax.broadcasted_iota(jnp.int32, (fine_share, w_up.shape[2]), 0)
    col = lax.broadcasted_iota(jnp.int32, (fine_share, w_up.shape[2]), 1)
    pick_up = jnp.where(col == rank * fine_share + row, 1.0, 0.0).astype(BF16)
    up_t[...] = jnp.concatenate(
        [
            lax.dot_general(
                pick_up, w_up[o], (((1,), (1,)), ((), ())), preferred_element_type=F32
            )
            for o in range(8)
        ],
        axis=0,
    ).astype(BF16)
    mid = w_mid[...].astype(F32)
    ordered = []
    for l in range(2):
        for ch in range(chunks):
            for h in range(2):
                at = (2 * h + l) * chunks * ROWS + ch * ROWS
                ordered.append(mid[at : at + ROWS])
    mid_t[...] = jnp.concatenate(ordered, axis=0).T.astype(BF16)

    for ch in range(chunks):
        whole(going, arrived, go_s, go_r, ch).wait_recv()
        spread(
            twice, ch, arrived[ch].astype(F32).reshape(half * ROWS, LANES), half
        )

        def paired(d, ch=ch):
            sums = []
            for m in range(per_dest):
                t = d * capacity + 2 * m
                own = arrived[ch, d, m].astype(F32)
                sums.append(
                    (own + joined(twice, ch, index[1, t], index[1, t + 1])).astype(BF16)
                )
            return sums

        def send_back(off, carry, ch=ch, paired=paired):
            d = mate(off)
            for m, value in enumerate(paired(d)):
                back[ch, d, m] = value
            exchange(back, returned, back_s, back_r, ch, d).start()
            return carry

        lax.fori_loop(1, n, send_back, 0, unroll=n - 1 if n <= 8 else 1)
        for m, value in enumerate(paired(me)):
            returned[ch, me, m] = value

    parts = 2
    span = pairs // parts
    shares, alls = [], []
    for ch in range(chunks):
        for p in range(parts):
            at, sem = pl.ds(p * span, span), ch * parts + p
            own = full.at[lo, ch, hi, at]
            shares.append(to(own, own, share_s.at[sem], share_r.at[sem], me, x_peer))
            both = full.at[lo, ch, :, at]
            alls.append(to(both, both, all_s.at[sem], all_r.at[sem], me, core_peer))

    def pass_on(ch):
        for i in range(ch * parts, (ch + 1) * parts):
            shares[i].wait_recv()
            alls[i].start()

    for ch in range(chunks):
        whole(back, returned, back_s, back_r, ch).wait_recv()
        spread(again, ch, returned[ch].astype(F32).reshape(half * ROWS, LANES), half)

        def collect(m, carry, ch=ch):
            full[lo, ch, hi, m] = joined(again, ch, index[2, 2 * m], index[2, 2 * m + 1]).astype(BF16)
            return carry

        for p in range(parts):
            lax.fori_loop(p * span, (p + 1) * span, collect, 0, unroll=8)
            shares[ch * parts + p].start()
        if ch > 0:
            pass_on(ch - 1)
    pass_on(chunks - 1)

    def up(step, carry):
        x = jnp.concatenate(
            [full[:, :, :, step * 2 + u].reshape(width, LANES) for u in range(2)], axis=1
        )
        coarse = jnp.dot(mid_t[...], x, preferred_element_type=F32).astype(BF16)
        lifted = jnp.dot(up_t[...], coarse, preferred_element_type=F32)
        for u in range(2):
            mine = lifted[:, u * LANES : (u + 1) * LANES]
            swapped = swap(mine)
            for b in range(2):
                j = step * 4 + 2 * u + b
                first, second = (mine, swapped) if b == 0 else (swapped, mine)
                for a in range(4):
                    r0, r1 = 2 * a * fine_share, (2 * a + 1) * fine_share
                    value = jnp.where(
                        left, first[r0 : r0 + fine_share], second[r1 : r1 + fine_share]
                    )
                    at = pl.ds(a * LANES, LANES)
                    tiles[j, :, at] = (tiles[j, :, at].astype(F32) + value).astype(BF16)
        return carry

    stores = []
    for p in range(pieces_in):
        if p % (pieces_in // parts) == 0:
            for ch in range(chunks):
                alls[ch * parts + p // (pieces_in // parts)].wait_recv()
        lax.fori_loop(p * piece // 4, (p + 1) * piece // 4, up, 0, unroll=2)
        at = pl.ds(p * piece, piece)
        stores.append(pltpu.make_async_copy(tiles.at[at], out.at[at], store_s.at[p]))
        stores[p].start()

    for ch in range(chunks):
        cores[ch].wait_send()
        xs[ch].wait_send()
        whole(going, arrived, go_s, go_r, ch).wait_send()
        whole(back, returned, back_s, back_r, ch).wait_send()
    for copy in shares + alls:
        copy.wait_send()
    for store in stores:
        store.wait()


def local(fine_tiles, parent_route, parent_slots, w_down, coarse_bias, w_mid, w_up):
    n = lax.axis_size("space")
    blocks = fine_tiles.shape[0]
    pairs = blocks // 2
    width = w_down.shape[2]
    slot_count = parent_slots.shape[0] * 8
    capacity = slot_count // n
    per_dest = capacity // 2
    half = slot_count // 2
    chunks = width // (4 * ROWS)
    hbm = pl.BlockSpec(memory_space=pltpu.HBM)
    lanes = -(-max(slot_count, blocks) // LANES) * LANES

    def buffer(*shape):
        return pltpu.VMEM(shape + (ROWS, LANES), BF16)

    return pl.pallas_call(
        functools.partial(main_kernel, n, capacity),
        out_shape=jax.ShapeDtypeStruct(fine_tiles.shape, fine_tiles.dtype),
        in_specs=[hbm] * 7,
        out_specs=hbm,
        scratch_shapes=[
            pltpu.VMEM(fine_tiles.shape, BF16),
            pltpu.VMEM(w_down.shape, BF16),
            pltpu.VMEM((1, width), F32),
            pltpu.VMEM(w_mid.shape, BF16),
            pltpu.VMEM(w_up.shape, BF16),
            pltpu.VMEM((1, blocks), jnp.int32),
            pltpu.VMEM(parent_slots.shape, jnp.int32),
            pltpu.VMEM((8, lanes), jnp.int32),
            pltpu.SMEM((8, lanes), jnp.int32),
            pltpu.SemaphoreType.DMA((10,)),
            pltpu.SemaphoreType.DMA((4,)),
            pltpu.SemaphoreType.DMA,
            pltpu.VMEM((2, width, LANES), BF16),
            pltpu.VMEM((width, width), BF16),
            pltpu.VMEM((8 * fine_tiles.shape[1], width), BF16),
            pltpu.VMEM((4 * chunks, ROWS, LANES), F32),
            buffer(2, chunks, 2, pairs),
            buffer(chunks, 2, pairs),
            buffer(chunks, pairs),
            buffer(chunks, pairs),
            buffer(chunks, 2 * pairs + 1),
            buffer(chunks, n, per_dest),
            buffer(chunks, n, per_dest),
            buffer(chunks, 2 * half),
            buffer(chunks, n, per_dest),
            buffer(chunks, n, per_dest),
            buffer(chunks, 2 * half),
            buffer(2, chunks, 2, pairs),
        ]
        + [pltpu.SemaphoreType.DMA((chunks,))] * 8
        + [pltpu.SemaphoreType.DMA((2 * chunks,))] * 4,
        compiler_params=pltpu.CompilerParams(
            collective_id=0, has_side_effects=True, vmem_limit_bytes=62 * 1024 * 1024
        ),
    )(
        parent_route.reshape(1, blocks),
        parent_slots,
        fine_tiles,
        w_down,
        coarse_bias.reshape(1, width),
        w_mid,
        w_up,
    )


def solution(mesh):
    in_specs = (P("space", "chan", None), P("space", None), P("space", None), P(), P(), P(), P())
    out_specs = P("space", "chan", None)
    return jax.shard_map(local, mesh=mesh, in_specs=in_specs, out_specs=out_specs, check_vma=False)
```

```python
import functools

import jax
import jax.numpy as jnp
from jax import lax
from jax.experimental import pallas as pl
from jax.experimental.pallas import tpu as pltpu
from jax.sharding import PartitionSpec as P

MESH = pl.DeviceIdType.MESH
LANES = 128
ROWS = 16
BF16 = jnp.bfloat16
F32 = jnp.float32


def build_tables(n, capacity, route, slots, tables):
    blocks = route.shape[1]
    pairs = blocks // 2
    half = n * capacity // 2
    lanes = tables.shape[1]

    def place(slot):
        return (slot % 2) * half + slot // 2

    j_row = lax.broadcasted_iota(jnp.int32, (blocks, blocks), 0)
    j_col = lax.broadcasted_iota(jnp.int32, (blocks, blocks), 1)
    row = jnp.broadcast_to(route[...], (blocks, blocks))
    own = jnp.sum(jnp.where(j_row == j_col, row, 0), axis=1, keepdims=True)
    earlier = jnp.where((row == own) & (j_col < j_row), 1, 0)
    slot = own * capacity + jnp.sum(earlier, axis=1, keepdims=True)
    j = lax.broadcasted_iota(jnp.int32, (blocks, lanes), 0)
    t = lax.broadcasted_iota(jnp.int32, (blocks, lanes), 1)
    named = jnp.where(slot == t, (j % 2) * pairs + j // 2 - 2 * pairs, 0)
    tables[...] = jnp.zeros_like(tables)
    tables[0:1] = jnp.sum(named, axis=0, keepdims=True) + 2 * pairs
    tables[2:3] = jnp.sum(jnp.where(j == t, place(slot), 0), axis=0, keepdims=True)
    t = lax.broadcasted_iota(jnp.int32, (slots.shape[0], lanes), 1)
    partner = jnp.zeros((slots.shape[0], lanes), jnp.int32)
    for q in range(8):
        mate = q + 1 - 2 * (q % 2)
        partner += jnp.where(slots[:, q : q + 1] == t, place(slots[:, mate : mate + 1]), 0)
    tables[1:2] = jnp.sum(partner, axis=0, keepdims=True)


def main_kernel(
    n, capacity, route_in, slots_in, tiles_in, down_in, bias_in, mid_in, up_in, out,
    tiles, w_down, bias, w_mid, w_up, route, slots, tables, index, load_s, store_s, table_s,
    down_t, mid_t, up_t, bias_t, part, core_in, x_out, x_in, acts, going, arrived, twice,
    back, returned, again, full, core_s, core_r, x_s, x_r, go_s, go_r, back_s, back_r,
    share_s, share_r, all_s, all_r,
):
    blocks, fine_share, voxels = tiles.shape
    pieces_in = 2
    piece = blocks // pieces_in
    sources = [(down_in, w_down), (route_in, route), (slots_in, slots)]
    for p in range(pieces_in):
        at = pl.ds(p * piece, piece)
        sources.append((tiles_in.at[at], tiles.at[at]))
    sources += [(bias_in, bias), (mid_in, w_mid), (up_in, w_up)]
    loads = [
        pltpu.make_async_copy(src, dst, load_s.at[i]) for i, (src, dst) in enumerate(sources)
    ]
    for load in loads:
        load.start()
    pairs = blocks // 2
    width = w_down.shape[2]
    chunks = part.shape[1]
    per_dest = capacity // 2
    half = n * per_dest
    me = lax.axis_index("space")
    rank = lax.axis_index("chan")
    hi, lo = rank // 2, rank % 2
    core_peer = 2 * hi + 1 - lo
    x_peer = 2 * (1 - hi) + lo

    barrier = pltpu.get_barrier_semaphore()

    def greet(off, carry):
        pl.semaphore_signal(
            barrier, inc=1, device_id=(lax.rem(me + off, n), rank), device_id_type=MESH
        )
        return carry

    lax.fori_loop(1, n, greet, 0)
    for peer in (core_peer, x_peer):
        pl.semaphore_signal(barrier, inc=1, device_id=(me, peer), device_id_type=MESH)

    left = lax.broadcasted_iota(jnp.int32, (1, LANES), 1) < LANES // 2

    def swap(v):
        return pltpu.roll(v, LANES // 2, 1)

    pad = 32
    row = lax.broadcasted_iota(jnp.int32, (pad, w_down.shape[1]), 0)
    col = lax.broadcasted_iota(jnp.int32, (pad, w_down.shape[1]), 1)
    loads[1].wait()
    loads[2].wait()
    build_tables(n, capacity, route, slots, tables)
    table_copy = pltpu.make_async_copy(tables, index, table_s)
    table_copy.start()
    loads[0].wait()
    pick = jnp.where((row < fine_share) & (col == rank * fine_share + row), 1.0, 0.0).astype(BF16)
    for parity in range(2):
        stacked = jnp.concatenate(
            [
                jnp.dot(pick, w_down[2 * a + parity], preferred_element_type=F32)
                for a in range(4)
            ],
            axis=0,
        )
        down_t[parity] = stacked.T.astype(BF16)

    zeros = jnp.zeros((pad - fine_share, LANES), F32)

    def down(step, carry):
        columns = []
        for b in range(4):
            tile = tiles[step * 4 + b].astype(F32)
            pieces = []
            for a in range(4):
                pieces += [tile[:, a * LANES : (a + 1) * LANES], zeros]
            columns.append(jnp.concatenate(pieces, axis=0).astype(BF16))
        x = jnp.concatenate(columns, axis=1)
        even = jnp.dot(down_t[0], x, preferred_element_type=F32)
        odd = jnp.dot(down_t[1], x, preferred_element_type=F32)
        for u in range(2):
            e0, e1 = even[:, 2 * u * LANES :][:, :LANES], even[:, (2 * u + 1) * LANES :][:, :LANES]
            o0, o1 = odd[:, 2 * u * LANES :][:, :LANES], odd[:, (2 * u + 1) * LANES :][:, :LANES]
            both = (jnp.where(left, e0, o1) + swap(jnp.where(left, e1, o0))).astype(BF16)
            for h in range(2):
                for l in range(2):
                    for ch in range(chunks):
                        at = (2 * h + l) * chunks * ROWS + ch * ROWS
                        part[l, ch, h, step * 2 + u] = both[at : at + ROWS]
        return carry

    for p in range(pieces_in):
        loads[3 + p].wait()
        lax.fori_loop(p * piece // 4, (p + 1) * piece // 4, down, 0, unroll=4)

    pl.semaphore_wait(barrier, n + 1)

    def to(src, dst, send, recv, space, chan):
        return pltpu.make_async_remote_copy(
            src_ref=src, dst_ref=dst, send_sem=send, recv_sem=recv,
            device_id=(space, chan), device_id_type=MESH,
        )

    cores = [
        to(part.at[1 - lo, ch], core_in.at[ch], core_s.at[ch], core_r.at[ch], me, core_peer)
        for ch in range(chunks)
    ]
    for copy in cores:
        copy.start()

    loads[3 + pieces_in].wait()
    bias_t[...] = jnp.broadcast_to(bias[...], (LANES, width)).T.reshape(
        4 * chunks, ROWS, LANES
    )

    xs = [to(x_out.at[ch], x_in.at[ch], x_s.at[ch], x_r.at[ch], me, x_peer) for ch in range(chunks)]
    for ch in range(chunks):
        cores[ch].wait_recv()
        x_out[ch] = (
            part[lo, ch, 1 - hi].astype(F32) + core_in[ch, 1 - hi].astype(F32)
        ).astype(BF16)
        xs[ch].start()

    def silu(v):
        return v / (1.0 + jnp.exp(-v))

    def spread(ref, ch, flat, count):
        swapped = swap(flat)
        ref[ch, 0:count] = jnp.where(left, flat, swapped).astype(BF16).reshape(count, ROWS, LANES)
        ref[ch, count : 2 * count] = (
            jnp.where(left, swapped, flat).astype(BF16).reshape(count, ROWS, LANES)
        )

    def joined(ref, ch, first, second):
        return jnp.where(left, ref[ch, first].astype(F32), ref[ch, second].astype(F32))

    def exchange(src, dst, send, recv, ch, d):
        return to(src.at[ch, d], dst.at[ch, me], send.at[ch], recv.at[ch], d, rank)

    other = lax.rem(me + 1, n)

    def whole(src, dst, send, recv, ch):
        return to(
            src.at[ch, pl.ds(0, n - 1)], dst.at[ch, pl.ds(0, n - 1)], send.at[ch], recv.at[ch],
            other, rank,
        )

    table_copy.wait()
    for ch in range(chunks):
        xs[ch].wait_recv()
        b = bias_t[rank * chunks + ch]
        total = (
            part[lo, ch, hi].astype(F32)
            + core_in[ch, hi].astype(F32)
            + x_in[ch].astype(F32)
            + b[None]
        )
        spread(acts, ch, silu(total).reshape(pairs * ROWS, LANES), pairs)
        acts[ch, 2 * pairs] = silu(b).astype(BF16)

        def send(off, carry, ch=ch):
            d = lax.rem(me + off, n)
            for m in range(per_dest):
                t = d * capacity + 2 * m
                going[ch, d, m] = joined(acts, ch, index[0, t], index[0, t + 1]).astype(BF16)
            exchange(going, arrived, go_s, go_r, ch, d).start()
            return carry

        lax.fori_loop(1, n, send, 0, unroll=n - 1 if n <= 8 else 1)
        for m in range(per_dest):
            t = me * capacity + 2 * m
            arrived[ch, me, m] = joined(acts, ch, index[0, t], index[0, t + 1]).astype(BF16)

    loads[4 + pieces_in].wait()
    loads[5 + pieces_in].wait()
    row = lax.broadcasted_iota(jnp.int32, (fine_share, w_up.shape[2]), 0)
    col = lax.broadcasted_iota(jnp.int32, (fine_share, w_up.shape[2]), 1)
    pick_up = jnp.where(col == rank * fine_share + row, 1.0, 0.0).astype(BF16)
    up_t[...] = jnp.concatenate(
        [
            lax.dot_general(
                pick_up, w_up[o], (((1,), (1,)), ((), ())), preferred_element_type=F32
            )
            for o in range(8)
        ],
        axis=0,
    ).astype(BF16)
    mid = w_mid[...].astype(F32)
    ordered = []
    for l in range(2):
        for ch in range(chunks):
            for h in range(2):
                at = (2 * h + l) * chunks * ROWS + ch * ROWS
                ordered.append(mid[at : at + ROWS])
    mid_t[...] = jnp.concatenate(ordered, axis=0).T.astype(BF16)

    for ch in range(chunks):
        whole(going, arrived, go_s, go_r, ch).wait_recv()
        spread(
            twice, ch, arrived[ch].astype(F32).reshape(half * ROWS, LANES), half
        )

        def paired(d, ch=ch):
            sums = []
            for m in range(per_dest):
                t = d * capacity + 2 * m
                own = arrived[ch, d, m].astype(F32)
                sums.append(
                    (own + joined(twice, ch, index[1, t], index[1, t + 1])).astype(BF16)
                )
            return sums

        def send_back(off, carry, ch=ch, paired=paired):
            d = lax.rem(me + off, n)
            for m, value in enumerate(paired(d)):
                back[ch, d, m] = value
            exchange(back, returned, back_s, back_r, ch, d).start()
            return carry

        lax.fori_loop(1, n, send_back, 0, unroll=n - 1 if n <= 8 else 1)
        for m, value in enumerate(paired(me)):
            returned[ch, me, m] = value

    parts = 2
    span = pairs // parts
    shares, alls = [], []
    for ch in range(chunks):
        for p in range(parts):
            at, sem = pl.ds(p * span, span), ch * parts + p
            own = full.at[lo, ch, hi, at]
            shares.append(to(own, own, share_s.at[sem], share_r.at[sem], me, x_peer))
            both = full.at[lo, ch, :, at]
            alls.append(to(both, both, all_s.at[sem], all_r.at[sem], me, core_peer))

    def pass_on(ch):
        for i in range(ch * parts, (ch + 1) * parts):
            shares[i].wait_recv()
            alls[i].start()

    for ch in range(chunks):
        whole(back, returned, back_s, back_r, ch).wait_recv()
        spread(again, ch, returned[ch].astype(F32).reshape(half * ROWS, LANES), half)

        def collect(m, carry, ch=ch):
            full[lo, ch, hi, m] = joined(again, ch, index[2, 2 * m], index[2, 2 * m + 1]).astype(BF16)
            return carry

        for p in range(parts):
            lax.fori_loop(p * span, (p + 1) * span, collect, 0, unroll=8)
            shares[ch * parts + p].start()
        if ch > 0:
            pass_on(ch - 1)
    pass_on(chunks - 1)

    def up(step, carry):
        x = jnp.concatenate(
            [full[:, :, :, step * 2 + u].reshape(width, LANES) for u in range(2)], axis=1
        )
        coarse = jnp.dot(mid_t[...], x, preferred_element_type=F32).astype(BF16)
        lifted = jnp.dot(up_t[...], coarse, preferred_element_type=F32)
        for u in range(2):
            mine = lifted[:, u * LANES : (u + 1) * LANES]
            swapped = swap(mine)
            for b in range(2):
                j = step * 4 + 2 * u + b
                first, second = (mine, swapped) if b == 0 else (swapped, mine)
                for a in range(4):
                    r0, r1 = 2 * a * fine_share, (2 * a + 1) * fine_share
                    value = jnp.where(
                        left, first[r0 : r0 + fine_share], second[r1 : r1 + fine_share]
                    )
                    at = pl.ds(a * LANES, LANES)
                    tiles[j, :, at] = (tiles[j, :, at].astype(F32) + value).astype(BF16)
        return carry

    stores = []
    for p in range(pieces_in):
        if p % (pieces_in // parts) == 0:
            for ch in range(chunks):
                alls[ch * parts + p // (pieces_in // parts)].wait_recv()
        lax.fori_loop(p * piece // 4, (p + 1) * piece // 4, up, 0, unroll=4)
        at = pl.ds(p * piece, piece)
        stores.append(pltpu.make_async_copy(tiles.at[at], out.at[at], store_s.at[p]))
        stores[p].start()

    for ch in range(chunks):
        cores[ch].wait_send()
        xs[ch].wait_send()
        whole(going, arrived, go_s, go_r, ch).wait_send()
        whole(back, returned, back_s, back_r, ch).wait_send()
    for copy in shares + alls:
        copy.wait_send()
    for store in stores:
        store.wait()


def local(fine_tiles, parent_route, parent_slots, w_down, coarse_bias, w_mid, w_up):
    n = lax.axis_size("space")
    blocks = fine_tiles.shape[0]
    pairs = blocks // 2
    width = w_down.shape[2]
    slot_count = parent_slots.shape[0] * 8
    capacity = slot_count // n
    per_dest = capacity // 2
    half = slot_count // 2
    chunks = width // (4 * ROWS)
    hbm = pl.BlockSpec(memory_space=pltpu.HBM)
    lanes = -(-max(slot_count, blocks) // LANES) * LANES

    def buffer(*shape):
        return pltpu.VMEM(shape + (ROWS, LANES), BF16)

    return pl.pallas_call(
        functools.partial(main_kernel, n, capacity),
        out_shape=jax.ShapeDtypeStruct(fine_tiles.shape, fine_tiles.dtype),
        in_specs=[hbm] * 7,
        out_specs=hbm,
        scratch_shapes=[
            pltpu.VMEM(fine_tiles.shape, BF16),
            pltpu.VMEM(w_down.shape, BF16),
            pltpu.VMEM((1, width), F32),
            pltpu.VMEM(w_mid.shape, BF16),
            pltpu.VMEM(w_up.shape, BF16),
            pltpu.VMEM((1, blocks), jnp.int32),
            pltpu.VMEM(parent_slots.shape, jnp.int32),
            pltpu.VMEM((8, lanes), jnp.int32),
            pltpu.SMEM((8, lanes), jnp.int32),
            pltpu.SemaphoreType.DMA((8,)),
            pltpu.SemaphoreType.DMA((2,)),
            pltpu.SemaphoreType.DMA,
            pltpu.VMEM((2, width, LANES), BF16),
            pltpu.VMEM((width, width), BF16),
            pltpu.VMEM((8 * fine_tiles.shape[1], width), BF16),
            pltpu.VMEM((4 * chunks, ROWS, LANES), F32),
            buffer(2, chunks, 2, pairs),
            buffer(chunks, 2, pairs),
            buffer(chunks, pairs),
            buffer(chunks, pairs),
            buffer(chunks, 2 * pairs + 1),
            buffer(chunks, n, per_dest),
            buffer(chunks, n, per_dest),
            buffer(chunks, 2 * half),
            buffer(chunks, n, per_dest),
            buffer(chunks, n, per_dest),
            buffer(chunks, 2 * half),
            buffer(2, chunks, 2, pairs),
        ]
        + [pltpu.SemaphoreType.DMA((chunks,))] * 8
        + [pltpu.SemaphoreType.DMA((2 * chunks,))] * 4,
        compiler_params=pltpu.CompilerParams(
            collective_id=0, has_side_effects=True, vmem_limit_bytes=62 * 1024 * 1024
        ),
    )(
        parent_route.reshape(1, blocks),
        parent_slots,
        fine_tiles,
        w_down,
        coarse_bias.reshape(1, width),
        w_mid,
        w_up,
    )


def solution(mesh):
    in_specs = (P("space", "chan", None), P("space", None), P("space", None), P(), P(), P(), P())
    out_specs = P("space", "chan", None)
    return jax.shard_map(local, mesh=mesh, in_specs=in_specs, out_specs=out_specs, check_vma=False)
```

```python
import functools

import jax
import jax.numpy as jnp
from jax import lax
from jax.experimental import pallas as pl
from jax.experimental.pallas import tpu as pltpu
from jax.sharding import PartitionSpec as P

MESH = pl.DeviceIdType.MESH
LANES = 128
ROWS = 16
BF16 = jnp.bfloat16
F32 = jnp.float32


def build_tables(n, capacity, route, slots, tables):
    blocks = route.shape[1]
    pairs = blocks // 2
    half = n * capacity // 2
    lanes = tables.shape[1]

    def place(slot):
        return (slot % 2) * half + slot // 2

    j_row = lax.broadcasted_iota(jnp.int32, (blocks, blocks), 0)
    j_col = lax.broadcasted_iota(jnp.int32, (blocks, blocks), 1)
    row = jnp.broadcast_to(route[...], (blocks, blocks))
    own = jnp.sum(jnp.where(j_row == j_col, row, 0), axis=1, keepdims=True)
    earlier = jnp.where((row == own) & (j_col < j_row), 1, 0)
    slot = own * capacity + jnp.sum(earlier, axis=1, keepdims=True)
    j = lax.broadcasted_iota(jnp.int32, (blocks, lanes), 0)
    t = lax.broadcasted_iota(jnp.int32, (blocks, lanes), 1)
    named = jnp.where(slot == t, (j % 2) * pairs + j // 2 - 2 * pairs, 0)
    tables[...] = jnp.zeros_like(tables)
    tables[0:1] = jnp.sum(named, axis=0, keepdims=True) + 2 * pairs
    tables[2:3] = jnp.sum(jnp.where(j == t, place(slot), 0), axis=0, keepdims=True)
    t = lax.broadcasted_iota(jnp.int32, (slots.shape[0], lanes), 1)
    partner = jnp.zeros((slots.shape[0], lanes), jnp.int32)
    for q in range(8):
        mate = q + 1 - 2 * (q % 2)
        partner += jnp.where(slots[:, q : q + 1] == t, place(slots[:, mate : mate + 1]), 0)
    tables[1:2] = jnp.sum(partner, axis=0, keepdims=True)


def main_kernel(
    n, capacity, route_in, slots_in, tiles_in, down_in, bias_in, mid_in, up_in, out,
    tiles, w_down, bias, w_mid, w_up, route, slots, tables, index, load_s, store_s, table_s,
    down_t, mid_t, up_t, bias_t, part, core_in, x_out, x_in, acts, going, arrived, twice,
    back, returned, again, full, core_s, core_r, x_s, x_r, go_s, go_r, back_s, back_r,
    share_s, share_r, all_s, all_r,
):
    blocks, fine_share, voxels = tiles.shape
    pieces_in = 2
    piece = blocks // pieces_in
    sources = [(down_in, w_down), (route_in, route), (slots_in, slots)]
    for p in range(pieces_in):
        at = pl.ds(p * piece, piece)
        sources.append((tiles_in.at[at], tiles.at[at]))
    sources += [(bias_in, bias), (mid_in, w_mid), (up_in, w_up)]
    loads = [
        pltpu.make_async_copy(src, dst, load_s.at[i]) for i, (src, dst) in enumerate(sources)
    ]
    for load in loads:
        load.start()
    pairs = blocks // 2
    width = w_down.shape[2]
    chunks = part.shape[1]
    per_dest = capacity // 2
    half = n * per_dest
    me = lax.axis_index("space")
    rank = lax.axis_index("chan")
    hi, lo = rank // 2, rank % 2
    core_peer = 2 * hi + 1 - lo
    x_peer = 2 * (1 - hi) + lo

    barrier = pltpu.get_barrier_semaphore()

    def greet(off, carry):
        pl.semaphore_signal(
            barrier, inc=1, device_id=(lax.rem(me + off, n), rank), device_id_type=MESH
        )
        return carry

    lax.fori_loop(1, n, greet, 0)
    for peer in (core_peer, x_peer):
        pl.semaphore_signal(barrier, inc=1, device_id=(me, peer), device_id_type=MESH)

    left = lax.broadcasted_iota(jnp.int32, (1, LANES), 1) < LANES // 2

    def swap(v):
        return pltpu.roll(v, LANES // 2, 1)

    pad = 32
    row = lax.broadcasted_iota(jnp.int32, (pad, w_down.shape[1]), 0)
    col = lax.broadcasted_iota(jnp.int32, (pad, w_down.shape[1]), 1)
    loads[1].wait()
    loads[2].wait()
    build_tables(n, capacity, route, slots, tables)
    table_copy = pltpu.make_async_copy(tables, index, table_s)
    table_copy.start()
    loads[0].wait()
    pick = jnp.where((row < fine_share) & (col == rank * fine_share + row), 1.0, 0.0).astype(BF16)
    for parity in range(2):
        stacked = jnp.concatenate(
            [
                jnp.dot(pick, w_down[2 * a + parity], preferred_element_type=F32)
                for a in range(4)
            ],
            axis=0,
        )
        down_t[parity] = stacked.T.astype(BF16)

    zeros = jnp.zeros((pad - fine_share, LANES), F32)

    def down(step, carry):
        columns = []
        for b in range(4):
            tile = tiles[step * 4 + b].astype(F32)
            pieces = []
            for a in range(4):
                pieces += [tile[:, a * LANES : (a + 1) * LANES], zeros]
            columns.append(jnp.concatenate(pieces, axis=0).astype(BF16))
        x = jnp.concatenate(columns, axis=1)
        even = jnp.dot(down_t[0], x, preferred_element_type=F32)
        odd = jnp.dot(down_t[1], x, preferred_element_type=F32)
        for u in range(2):
            e0, e1 = even[:, 2 * u * LANES :][:, :LANES], even[:, (2 * u + 1) * LANES :][:, :LANES]
            o0, o1 = odd[:, 2 * u * LANES :][:, :LANES], odd[:, (2 * u + 1) * LANES :][:, :LANES]
            both = (jnp.where(left, e0, o1) + swap(jnp.where(left, e1, o0))).astype(BF16)
            for h in range(2):
                for l in range(2):
                    for ch in range(chunks):
                        at = (2 * h + l) * chunks * ROWS + ch * ROWS
                        part[l, ch, h, step * 2 + u] = both[at : at + ROWS]
        return carry

    def to(src, dst, send, recv, space, chan):
        return pltpu.make_async_remote_copy(
            src_ref=src, dst_ref=dst, send_sem=send, recv_sem=recv,
            device_id=(space, chan), device_id_type=MESH,
        )

    cores = []
    for p in range(pieces_in):
        loads[3 + p].wait()
        lax.fori_loop(p * piece // 4, (p + 1) * piece // 4, down, 0, unroll=4)
        if p == 0:
            pl.semaphore_wait(barrier, n + 1)
        at = pl.ds(p * piece // 2, piece // 2)
        for ch in range(chunks):
            i = p * chunks + ch
            cores.append(
                to(part.at[1 - lo, ch, :, at], core_in.at[ch, :, at], core_s.at[i], core_r.at[i],
                   me, core_peer)
            )
            cores[i].start()

    loads[3 + pieces_in].wait()
    bias_t[...] = jnp.broadcast_to(bias[...], (LANES, width)).T.reshape(
        4 * chunks, ROWS, LANES
    )

    xs = [to(x_out.at[ch], x_in.at[ch], x_s.at[ch], x_r.at[ch], me, x_peer) for ch in range(chunks)]
    for ch in range(chunks):
        for copy in cores[ch::chunks]:
            copy.wait_recv()
        x_out[ch] = (
            part[lo, ch, 1 - hi].astype(F32) + core_in[ch, 1 - hi].astype(F32)
        ).astype(BF16)
        xs[ch].start()

    def silu(v):
        return v / (1.0 + jnp.exp(-v))

    def spread(ref, ch, flat, count):
        swapped = swap(flat)
        ref[ch, 0:count] = jnp.where(left, flat, swapped).astype(BF16).reshape(count, ROWS, LANES)
        ref[ch, count : 2 * count] = (
            jnp.where(left, swapped, flat).astype(BF16).reshape(count, ROWS, LANES)
        )

    def joined(ref, ch, first, second):
        return jnp.where(left, ref[ch, first].astype(F32), ref[ch, second].astype(F32))

    def exchange(src, dst, send, recv, ch, d):
        return to(src.at[ch, d], dst.at[ch, me], send.at[ch], recv.at[ch], d, rank)

    other = lax.rem(me + 1, n)

    def whole(src, dst, send, recv, ch):
        return to(
            src.at[ch, pl.ds(0, n - 1)], dst.at[ch, pl.ds(0, n - 1)], send.at[ch], recv.at[ch],
            other, rank,
        )

    table_copy.wait()
    for ch in range(chunks):
        xs[ch].wait_recv()
        b = bias_t[rank * chunks + ch]
        total = (
            part[lo, ch, hi].astype(F32)
            + core_in[ch, hi].astype(F32)
            + x_in[ch].astype(F32)
            + b[None]
        )
        spread(acts, ch, silu(total).reshape(pairs * ROWS, LANES), pairs)
        acts[ch, 2 * pairs] = silu(b).astype(BF16)

        def send(off, carry, ch=ch):
            d = lax.rem(me + off, n)
            for m in range(per_dest):
                t = d * capacity + 2 * m
                going[ch, d, m] = joined(acts, ch, index[0, t], index[0, t + 1]).astype(BF16)
            exchange(going, arrived, go_s, go_r, ch, d).start()
            return carry

        lax.fori_loop(1, n, send, 0, unroll=n - 1 if n <= 8 else 1)
        for m in range(per_dest):
            t = me * capacity + 2 * m
            arrived[ch, me, m] = joined(acts, ch, index[0, t], index[0, t + 1]).astype(BF16)

    loads[4 + pieces_in].wait()
    loads[5 + pieces_in].wait()
    row = lax.broadcasted_iota(jnp.int32, (fine_share, w_up.shape[2]), 0)
    col = lax.broadcasted_iota(jnp.int32, (fine_share, w_up.shape[2]), 1)
    pick_up = jnp.where(col == rank * fine_share + row, 1.0, 0.0).astype(BF16)
    up_t[...] = jnp.concatenate(
        [
            lax.dot_general(
                pick_up, w_up[o], (((1,), (1,)), ((), ())), preferred_element_type=F32
            )
            for o in range(8)
        ],
        axis=0,
    ).astype(BF16)
    mid = w_mid[...].astype(F32)
    ordered = []
    for l in range(2):
        for ch in range(chunks):
            for h in range(2):
                at = (2 * h + l) * chunks * ROWS + ch * ROWS
                ordered.append(mid[at : at + ROWS])
    mid_t[...] = jnp.concatenate(ordered, axis=0).T.astype(BF16)

    for ch in range(chunks):
        whole(going, arrived, go_s, go_r, ch).wait_recv()
        spread(
            twice, ch, arrived[ch].astype(F32).reshape(half * ROWS, LANES), half
        )

        def paired(d, ch=ch):
            sums = []
            for m in range(per_dest):
                t = d * capacity + 2 * m
                own = arrived[ch, d, m].astype(F32)
                sums.append(
                    (own + joined(twice, ch, index[1, t], index[1, t + 1])).astype(BF16)
                )
            return sums

        def send_back(off, carry, ch=ch, paired=paired):
            d = lax.rem(me + off, n)
            for m, value in enumerate(paired(d)):
                back[ch, d, m] = value
            exchange(back, returned, back_s, back_r, ch, d).start()
            return carry

        lax.fori_loop(1, n, send_back, 0, unroll=n - 1 if n <= 8 else 1)
        for m, value in enumerate(paired(me)):
            returned[ch, me, m] = value

    parts = 2
    span = pairs // parts
    shares, alls = [], []
    for ch in range(chunks):
        for p in range(parts):
            at, sem = pl.ds(p * span, span), ch * parts + p
            own = full.at[lo, ch, hi, at]
            shares.append(to(own, own, share_s.at[sem], share_r.at[sem], me, x_peer))
            both = full.at[lo, ch, :, at]
            alls.append(to(both, both, all_s.at[sem], all_r.at[sem], me, core_peer))

    def pass_on(ch):
        for i in range(ch * parts, (ch + 1) * parts):
            shares[i].wait_recv()
            alls[i].start()

    for ch in range(chunks):
        whole(back, returned, back_s, back_r, ch).wait_recv()
        spread(again, ch, returned[ch].astype(F32).reshape(half * ROWS, LANES), half)

        def collect(m, carry, ch=ch):
            full[lo, ch, hi, m] = joined(again, ch, index[2, 2 * m], index[2, 2 * m + 1]).astype(BF16)
            return carry

        for p in range(parts):
            lax.fori_loop(p * span, (p + 1) * span, collect, 0, unroll=8)
            shares[ch * parts + p].start()
        if ch > 0:
            pass_on(ch - 1)
    pass_on(chunks - 1)

    def up(step, carry):
        x = jnp.concatenate(
            [full[:, :, :, step * 2 + u].reshape(width, LANES) for u in range(2)], axis=1
        )
        coarse = jnp.dot(mid_t[...], x, preferred_element_type=F32).astype(BF16)
        lifted = jnp.dot(up_t[...], coarse, preferred_element_type=F32)
        for u in range(2):
            mine = lifted[:, u * LANES : (u + 1) * LANES]
            swapped = swap(mine)
            for b in range(2):
                j = step * 4 + 2 * u + b
                first, second = (mine, swapped) if b == 0 else (swapped, mine)
                for a in range(4):
                    r0, r1 = 2 * a * fine_share, (2 * a + 1) * fine_share
                    value = jnp.where(
                        left, first[r0 : r0 + fine_share], second[r1 : r1 + fine_share]
                    )
                    at = pl.ds(a * LANES, LANES)
                    tiles[j, :, at] = (tiles[j, :, at].astype(F32) + value).astype(BF16)
        return carry

    stores = []
    for p in range(pieces_in):
        if p % (pieces_in // parts) == 0:
            for ch in range(chunks):
                alls[ch * parts + p // (pieces_in // parts)].wait_recv()
        lax.fori_loop(p * piece // 4, (p + 1) * piece // 4, up, 0, unroll=4)
        at = pl.ds(p * piece, piece)
        stores.append(pltpu.make_async_copy(tiles.at[at], out.at[at], store_s.at[p]))
        stores[p].start()

    for ch in range(chunks):
        for copy in cores[ch::chunks]:
            copy.wait_send()
        xs[ch].wait_send()
        whole(going, arrived, go_s, go_r, ch).wait_send()
        whole(back, returned, back_s, back_r, ch).wait_send()
    for copy in shares + alls:
        copy.wait_send()
    for store in stores:
        store.wait()


def local(fine_tiles, parent_route, parent_slots, w_down, coarse_bias, w_mid, w_up):
    n = lax.axis_size("space")
    blocks = fine_tiles.shape[0]
    pairs = blocks // 2
    width = w_down.shape[2]
    slot_count = parent_slots.shape[0] * 8
    capacity = slot_count // n
    per_dest = capacity // 2
    half = slot_count // 2
    chunks = width // (4 * ROWS)
    hbm = pl.BlockSpec(memory_space=pltpu.HBM)
    lanes = -(-max(slot_count, blocks) // LANES) * LANES

    def buffer(*shape):
        return pltpu.VMEM(shape + (ROWS, LANES), BF16)

    return pl.pallas_call(
        functools.partial(main_kernel, n, capacity),
        out_shape=jax.ShapeDtypeStruct(fine_tiles.shape, fine_tiles.dtype),
        in_specs=[hbm] * 7,
        out_specs=hbm,
        scratch_shapes=[
            pltpu.VMEM(fine_tiles.shape, BF16),
            pltpu.VMEM(w_down.shape, BF16),
            pltpu.VMEM((1, width), F32),
            pltpu.VMEM(w_mid.shape, BF16),
            pltpu.VMEM(w_up.shape, BF16),
            pltpu.VMEM((1, blocks), jnp.int32),
            pltpu.VMEM(parent_slots.shape, jnp.int32),
            pltpu.VMEM((8, lanes), jnp.int32),
            pltpu.SMEM((8, lanes), jnp.int32),
            pltpu.SemaphoreType.DMA((8,)),
            pltpu.SemaphoreType.DMA((2,)),
            pltpu.SemaphoreType.DMA,
            pltpu.VMEM((2, width, LANES), BF16),
            pltpu.VMEM((width, width), BF16),
            pltpu.VMEM((8 * fine_tiles.shape[1], width), BF16),
            pltpu.VMEM((4 * chunks, ROWS, LANES), F32),
            buffer(2, chunks, 2, pairs),
            buffer(chunks, 2, pairs),
            buffer(chunks, pairs),
            buffer(chunks, pairs),
            buffer(chunks, 2 * pairs + 1),
            buffer(chunks, n, per_dest),
            buffer(chunks, n, per_dest),
            buffer(chunks, 2 * half),
            buffer(chunks, n, per_dest),
            buffer(chunks, n, per_dest),
            buffer(chunks, 2 * half),
            buffer(2, chunks, 2, pairs),
        ]
        + [pltpu.SemaphoreType.DMA((2 * chunks,))] * 2
        + [pltpu.SemaphoreType.DMA((chunks,))] * 6
        + [pltpu.SemaphoreType.DMA((2 * chunks,))] * 4,
        compiler_params=pltpu.CompilerParams(
            collective_id=0, has_side_effects=True, vmem_limit_bytes=62 * 1024 * 1024
        ),
    )(
        parent_route.reshape(1, blocks),
        parent_slots,
        fine_tiles,
        w_down,
        coarse_bias.reshape(1, width),
        w_mid,
        w_up,
    )


def solution(mesh):
    in_specs = (P("space", "chan", None), P("space", None), P("space", None), P(), P(), P(), P())
    out_specs = P("space", "chan", None)
    return jax.shard_map(local, mesh=mesh, in_specs=in_specs, out_specs=out_specs, check_vma=False)
```
